32 devices in a mesh: angle: 8 (over z, y), tile: 4 (over x, core).
Axes of the slice: x: 2, y: 2, z: 4, core: 2. Of those that a mesh axis runs over, the one named last changes fastest.
Arguments:
- projection: float32 [2, 8, 1024, 512], P(None, 'angle', 'tile'), may hold values from -5 to 5
- probe: float32 [2, 128, 128], replicated, may hold values from -5 to 5
- amplitude: float32 [8, 16, 128, 128], P('angle', 'tile'), may hold values from 0.4 to 2.2
- pos_row: int32 [8, 16], P('angle', 'tile'), may hold values from 0 to 255
- pos_col: int32 [8, 16], P('angle', 'tile'), may hold values from 0 to 384
- ang_offset: int32 [8], replicated, may hold values from 0 to 4, as said below
- ang_weight: float32 [8, 4], replicated, may hold values from 0.1 to 0.6
- det_offset: int32 [256], replicated, may hold values from 0 to 508, as said below
- det_weight: float32 [256, 4], replicated, may hold values from 0.1 to 0.6
Outputs:
- updated_projection: float32 [2, 8, 1024, 512], P(None, 'angle', 'tile')
- probe_direction: float32 [2, 128, 128], replicated
- volume: float32 [2, 4, 256, 8, 256], P(None, 'tile', 'angle')
The draws below stay inside these ranges and needn't reach their ends.
Inputs may be any that keep to these rules, and one draw needn't show every extreme that they name: `ang_offset`: regular angle r's band starts within one of r - 1, clipped to the valid range; both ends are reached. `det_offset`: radial sample q's band starts within one of 2 q - 1, clipped to the valid range; both ends are reached.
All inputs are finite; a program needn't handle non-finite values.
Results may differ from the reference program's by a relative error of at most 0.00011.
Values sent between devices are 32-bit elements; how exact they have to be, the bound alone decides.
A program may use at most 64 MiB of HBM per device.

```python
import math
import jax
import jax.numpy as jnp
from jax import lax

P_SIZE = 128
W = 512
TILE_ROWS = 256
PAT_DEV = 4
HALF = 64
ANGLES = 8
PATCHES = 16
H = 1024
NREG = 8
NR = 256
N_TILE = 4


def draw_ang_offset(key, part):
    jitter = jax.random.randint(key, (NREG,), -1, 2)
    base_rows = jnp.arange(NREG, dtype=jnp.int32) - 1 + jitter
    return jnp.clip(base_rows, 0, ANGLES - 4).astype(jnp.int32)


def draw_det_offset(key, part):
    jitter = jax.random.randint(jax.random.fold_in(key, 7), (NR,), -1, 2)
    base_rows = 2 * jnp.arange(NR, dtype=jnp.int32) - 1 + jitter
    return jnp.clip(base_rows, 0, W - 4).astype(jnp.int32)


def with_ends(array, own_key, smallest, high):
    longest = array.shape.index(max(array.shape))
    spots = []
    for shift in (0, 1):
        where = [jax.random.randint(jax.random.fold_in(own_key, axis), (), 0, length) for axis, length in enumerate(array.shape)]
        where[longest] = (where[longest] + shift) % array.shape[longest]
        spots.append(tuple(where))
    return array.at[spots[0]].set(smallest).at[spots[1]].set(high)


def level_of(rng, shape, cuts, smallest, top_value):
    def one(dim, parts):
        heights = jax.random.uniform(jax.random.fold_in(jax.random.fold_in(rng, 6), dim), (parts,), jnp.float32, smallest / len(cuts), top_value / len(cuts))
        return jnp.repeat(jnp.exp(heights), shape[dim] // parts).reshape((-1,) + (1,) * (len(shape) - dim - 1))

    level = one(*cuts[0])
    for cut in cuts[1:]:
        level = level * one(*cut)
    return level


def normal_values(stream_key, extent, width, limit, cuts=(), held_as=jnp.bfloat16):
    result = jax.random.normal(stream_key, extent, jnp.float32) * width
    if len(cuts) > 0:
        result = level_of(stream_key, extent, cuts, -0.22, 0.18) * result
    return jnp.clip(result, min=-limit, max=limit).astype(held_as)


def setup_inputs(seed: int = 0) -> dict:
    seeds = jax.random.split(jax.random.key(seed), 10)
    projection = normal_values(seeds[0], (2, ANGLES, H, W), 0.7, 5.0, ((1, 8), (2, 4)), jnp.float32)
    probe = normal_values(seeds[1], (2, P_SIZE, P_SIZE), 0.7, 5.0, (), jnp.float32)
    amplitude = jnp.clip(0.4 + 1.80000004 * jax.random.uniform(seeds[2], (ANGLES, PATCHES, P_SIZE, P_SIZE), jnp.float32) ** level_of(seeds[2], (ANGLES, PATCHES, P_SIZE, P_SIZE), ((0, 8), (1, 4)), -0.2, 0.2), 0.4, 2.2)
    pos_row = with_ends(jax.random.randint(seeds[3], (ANGLES, PATCHES), 0, TILE_ROWS), jax.random.fold_in(seeds[3], 1), 0, TILE_ROWS - 1).astype(jnp.int32)
    pos_col = with_ends(jax.random.randint(seeds[4], (ANGLES, PATCHES), 0, W - P_SIZE + 1), jax.random.fold_in(seeds[4], 1), 0, W - P_SIZE).astype(jnp.int32)
    ang_offset = draw_ang_offset(jax.random.fold_in(seeds[9], 71), 0)
    ang_weight = jnp.clip(jax.random.uniform(seeds[6], (NREG, 4), jnp.float32, 0.1, 0.6), 0.1, 0.6)
    det_offset = draw_det_offset(jax.random.fold_in(seeds[9], 71), 0)
    det_weight = jnp.clip(jax.random.uniform(seeds[8], (NR, 4), jnp.float32, 0.1, 0.6), 0.1, 0.6)
    return {"projection": projection, "probe": probe, "amplitude": amplitude, "pos_row": pos_row, "pos_col": pos_col, "ang_offset": ang_offset, "ang_weight": ang_weight, "det_offset": det_offset, "det_weight": det_weight}


STEP_SIZE = 0.1
EPSILON = 1e-06
HIGHEST = lax.Precision.HIGHEST

def dft_tables(length):
    counter = jnp.arange(length, dtype=jnp.int32)
    product_mod = counter[:, None] * counter[None, :] % length
    angle_table = product_mod.astype(jnp.float32) * (2.0 * math.pi / length)
    norm_scale = 1.0 / math.sqrt(length)
    return (jnp.cos(angle_table) * norm_scale, -jnp.sin(angle_table) * norm_scale)

def transform(values_re, values_im, table_re, table_im):
    left_re = jnp.einsum('ij,bjk->bik', table_re, values_re, precision=HIGHEST) - jnp.einsum('ij,bjk->bik', table_im, values_im, precision=HIGHEST)
    left_im = jnp.einsum('ij,bjk->bik', table_re, values_im, precision=HIGHEST) + jnp.einsum('ij,bjk->bik', table_im, values_re, precision=HIGHEST)
    right_re = jnp.einsum('bij,jk->bik', left_re, table_re, precision=HIGHEST) - jnp.einsum('bij,jk->bik', left_im, table_im, precision=HIGHEST)
    right_im = jnp.einsum('bij,jk->bik', left_re, table_im, precision=HIGHEST) + jnp.einsum('bij,jk->bik', left_im, table_re, precision=HIGHEST)
    return (right_re, right_im)

def patch_terms(object_re, object_im, amp_block, probe_re, probe_im, cosine_table, sine_table):
    exit_re = probe_re * object_re - probe_im * object_im
    exit_im = probe_re * object_im + probe_im * object_re
    spec_re, spec_im = transform(exit_re, exit_im, cosine_table, sine_table)
    magnitude = jnp.sqrt(spec_re * spec_re + spec_im * spec_im)
    factor = 1.0 - amp_block / jnp.maximum(magnitude, 1.0)
    back_re, back_im = transform(spec_re * factor, spec_im * factor, cosine_table, -sine_table)
    grad_re = probe_re * back_re + probe_im * back_im
    grad_im = probe_re * back_im - probe_im * back_re
    term_re = lax.optimization_barrier(jnp.sum(object_re * back_re + object_im * back_im, axis=0))
    term_im = lax.optimization_barrier(jnp.sum(object_re * back_im - object_im * back_re, axis=0))
    weight_sum = lax.optimization_barrier(jnp.sum(object_re * object_re + object_im * object_im, axis=0))
    return (grad_re, grad_im, term_re, term_im, weight_sum)

def band_matrix(offset, weight, length):
    columns = jnp.arange(length, dtype=jnp.int32)
    matrix = jnp.zeros((offset.shape[0], length), jnp.float32)
    for band_step in range(weight.shape[1]):
        hits = (columns[None, :] == offset[:, None] + band_step).astype(jnp.float32)
        matrix = matrix + weight[:, band_step:band_step + 1] * hits
    return matrix

def reference(projection, probe, amplitude, pos_row, pos_col, ang_offset, ang_weight, det_offset, det_weight):
    cosine_table, sine_table = dft_tables(P_SIZE)
    probe_re = probe[0]
    probe_im = probe[1]
    padded = jnp.pad(projection, ((0, 0), (0, 0), (HALF, HALF), (0, 0)))
    padded = jnp.moveaxis(padded, 1, 0)
    owners = jnp.arange(PATCHES, dtype=jnp.int32) // PAT_DEV

    def one_angle(carried, inputs):
        plane_data, row_here, col_here, amp_here = inputs
        starts = owners * TILE_ROWS + row_here

        def cut_patch(start_row, start_col):
            return lax.dynamic_slice(plane_data, (jnp.int32(0), start_row, start_col), (2, P_SIZE, P_SIZE))
        pieces = jax.vmap(cut_patch)(starts, col_here)
        grad_re, grad_im, term_re, term_im, weight_sum = patch_terms(pieces[:, 0], pieces[:, 1], amp_here, probe_re, probe_im, cosine_table, sine_table)

        def deposit(number, accumulated):
            corner = (jnp.int32(0), starts[number], col_here[number])
            window = lax.dynamic_slice(accumulated, corner, (2, P_SIZE, P_SIZE))
            addend = jnp.stack([grad_re[number], grad_im[number]])
            return lax.dynamic_update_slice(accumulated, window + addend, corner)
        gradient = lax.fori_loop(0, PATCHES, deposit, jnp.zeros_like(plane_data))
        summed = (carried[0] + term_re, carried[1] + term_im, carried[2] + weight_sum)
        return (summed, gradient)
    zeros_pp = jnp.zeros((P_SIZE, P_SIZE), jnp.float32)
    sums, stacked = lax.scan(one_angle, (zeros_pp, zeros_pp, zeros_pp), (padded, pos_row, pos_col, amplitude))
    gradient = jnp.moveaxis(stacked, 0, 1)[:, :, HALF:HALF + H]
    updated = projection - STEP_SIZE * gradient
    norm_scale = lax.rsqrt(sums[2] + EPSILON)
    direction = jnp.stack([sums[0] * norm_scale, sums[1] * norm_scale])
    det_matrix = band_matrix(det_offset, det_weight, W)
    ang_matrix = band_matrix(ang_offset, ang_weight, ANGLES)
    resampled = jnp.einsum('cahw,qw->cahq', updated, det_matrix, precision=HIGHEST)
    volume = jnp.einsum('ra,cahq->chrq', ang_matrix, resampled, precision=HIGHEST)
    volume = volume.reshape(2, N_TILE, TILE_ROWS, NREG, NR)
    return (updated, direction, volume)
```

```python
import functools
import math

import jax
import jax.numpy as jnp
import numpy as np
from jax import lax
from jax.experimental import pallas as pl
from jax.experimental.pallas import tpu as pltpu
from jax.sharding import PartitionSpec as P

STEP_SIZE = 0.1
EPSILON = 1e-06
MESH = pl.DeviceIdType.MESH
F32 = jnp.float32
BF16 = jnp.bfloat16


def dft_tables(length):
    counter = np.arange(length)
    angle = (counter[:, None] * counter[None, :] % length) * (2.0 * math.pi / length)
    re, im = np.cos(angle) / math.sqrt(length), -np.sin(angle) / math.sqrt(length)
    forward = np.block([[re, -im], [im, re]]).astype(np.float32)
    tables = []
    for table in (forward, forward.T):
        high = table.astype(jnp.bfloat16)
        tables += [high, (table - high.astype(np.float32)).astype(jnp.bfloat16)]
    return np.stack(tables)


def split(value):
    high = value.astype(BF16)
    return high, (value - high.astype(F32)).astype(BF16)


def dot3(left, right, transposed=False):
    dims = (((1,), (1 if transposed else 0,)), ((), ()))

    def one(a, b):
        return lax.dot_general(a, b, dims, preferred_element_type=F32)

    return one(left[0], right[0]) + (one(left[0], right[1]) + one(left[1], right[0]))


def chosen(shape, by, from_rows=False):
    i, j = (lax.broadcasted_iota(jnp.int32, shape, d) for d in range(2))
    return jnp.where(i == j + by if from_rows else j == i + by, 1.0, 0.0).astype(BF16)


def quotient(value, by):
    if by & (by - 1) == 0:
        return lax.shift_right_logical(value, jnp.int32(by.bit_length() - 1))
    return lax.div(value, jnp.int32(by))


def as_column(row, count):
    shape = (count, count)
    diagonal = lax.broadcasted_iota(jnp.int32, shape, 0) == lax.broadcasted_iota(jnp.int32, shape, 1)
    wide = jnp.broadcast_to(row.astype(F32)[None, :], shape)
    return jnp.sum(jnp.where(diagonal, wide, 0.0), axis=1, keepdims=True)


def banded(offset, weight, columns):
    matrix = None
    for step in range(weight.shape[1]):
        term = jnp.where(columns == offset + float(step), weight[:, step : step + 1], 0.0)
        matrix = term if matrix is None else matrix + term
    return matrix


def kernel(
    sizes,
    proj_ref,
    probe_ref,
    amp_ref,
    row_ref,
    col_ref,
    ang_off_ref,
    ang_w_ref,
    det_off_ref,
    det_w_ref,
    table_ref,
    upd_ref,
    dir_ref,
    vol_ref,
    pad,
    acc,
    from_above,
    from_below,
    det_hl,
    mix_hl,
    outbox,
    inbox,
    terms,
    terms_in,
    parts,
    parts_in,
    dirs,
    quarters,
    local_sem,
    halo_send,
    halo_recv,
    a2a_send,
    a2a_recv,
    t_send,
    t_recv,
    p_send,
    p_recv,
    d_send,
    d_recv,
    q_send,
    q_recv,
):
    n_ang, n_tile, side, rows, width, patches, n_reg, n_rad, slab, inside = sizes
    half = side // 2
    me_a, me_t = lax.axis_index("angle"), lax.axis_index("tile")
    first, last = me_t == 0, me_t == n_tile - 1
    barrier = pltpu.get_barrier_semaphore()

    def each_angle(body, low=0, high=n_ang):
        def step(i, carry):
            @pl.when(i != me_a)
            def _():
                body(i)

            return carry

        lax.fori_loop(low, high, step, 0)

    def each_tile(body):
        for j in range(n_tile):

            @pl.when(j != me_t)
            def _():
                body(j)

    def to(src, dst, send, recv, angle=None, tile=None):
        return pltpu.make_async_remote_copy(
            src_ref=src,
            dst_ref=dst,
            send_sem=send,
            recv_sem=recv,
            device_id=(me_a if angle is None else angle, me_t if tile is None else tile),
            device_id_type=MESH,
        )

    def hello(angle, tile):
        pl.semaphore_signal(barrier, inc=1, device_id=(angle, tile), device_id_type=MESH)

    each_tile(lambda j: hello(me_a, j))
    each_angle(lambda i: hello(i, me_t))
    own = pltpu.make_async_copy(proj_ref.at[:, 0], pad.at[:, half : half + rows], local_sem)
    own.start()
    pl.semaphore_wait(barrier, n_tile - 1 + n_ang - 1)

    up = to(proj_ref.at[:, 0, 0:half], pad.at[:, half + rows :], halo_send.at[0], halo_recv.at[0], tile=me_t - 1)
    down = to(
        proj_ref.at[:, 0, rows - half :], pad.at[:, 0:half], halo_send.at[1], halo_recv.at[1], tile=me_t + 1
    )
    pl.when(jnp.logical_not(first))(up.start)
    pl.when(jnp.logical_not(last))(down.start)

    @pl.when(first)
    def _():
        pad[:, 0:half] = jnp.zeros((2, half, width), F32)
        from_above[...] = jnp.zeros_like(from_above)

    @pl.when(last)
    def _():
        pad[:, half + rows :] = jnp.zeros((2, half, width), F32)
        from_below[...] = jnp.zeros_like(from_below)

    det_cols = lax.broadcasted_iota(jnp.int32, (n_rad, width), 1).astype(F32)
    det = split(banded(as_column(det_off_ref[...], n_rad), det_w_ref[...], det_cols))
    det_hl[0], det_hl[1] = det
    square = (slab * n_reg, n_ang * slab)
    wide_rows = lax.broadcasted_iota(jnp.int32, square, 0)
    wide_cols = lax.broadcasted_iota(jnp.int32, square, 1)
    source = quotient(wide_cols, slab)
    same = (wide_cols - source * slab) == quotient(wide_rows, n_reg)
    offs = jnp.concatenate([as_column(ang_off_ref[...], n_reg)] * slab, axis=0)
    weights = jnp.concatenate([ang_w_ref[...]] * slab, axis=0)
    mix = split(jnp.where(same, banded(offs, weights, source.astype(F32)), 0.0))
    mix_hl[0], mix_hl[1] = mix

    own.wait()
    pl.when(jnp.logical_not(last))(up.wait_recv)
    pl.when(jnp.logical_not(first))(down.wait_recv)

    probe_re, probe_im = probe_ref[0], probe_ref[1]
    objects, exits = [], []
    places = [(row_ref[0, k], col_ref[0, k]) for k in range(patches)]
    row_pick = jnp.concatenate([chosen((side, rows + side), row) for row, _ in places], axis=0)
    seen = jnp.concatenate([pad[0], pad[1]], axis=1)
    seen = [jnp.dot(row_pick, part, preferred_element_type=F32).astype(BF16) for part in split(seen)]
    for k, (_, col) in enumerate(places):
        here = slice(k * side, (k + 1) * side)
        strip = jnp.concatenate([part[here, c * width : (c + 1) * width] for part in seen for c in range(2)], axis=0)
        picked = jnp.dot(strip, chosen((width, side), col, True), preferred_element_type=F32)
        o_re, o_im = [picked[c * side : (c + 1) * side] + picked[(c + 2) * side : (c + 3) * side] for c in range(2)]
        objects.append((o_re, o_im))
        exits.append(
            jnp.concatenate([probe_re * o_re - probe_im * o_im, probe_re * o_im + probe_im * o_re], axis=0)
        )
    fwd = (table_ref[0], table_ref[1])
    bwd = (table_ref[2], table_ref[3])
    left = dot3(fwd, split(jnp.concatenate(exits, axis=1)))
    stacked = jnp.concatenate(
        [
            jnp.concatenate([left[:side, k * side : (k + 1) * side], left[side:, k * side : (k + 1) * side]], axis=1)
            for k in range(patches)
        ],
        axis=0,
    )
    spec = dot3(split(stacked), bwd)
    s_re, s_im = spec[:, :side], spec[:, side:]
    amp = amp_ref[0].reshape(patches * side, side)
    factor = 1.0 - amp / jnp.maximum(jnp.sqrt(s_re * s_re + s_im * s_im), 1.0)
    right = dot3(split(jnp.concatenate([s_re * factor, s_im * factor], axis=1)), fwd)
    regrouped = jnp.concatenate(
        [
            jnp.concatenate([right[k * side : (k + 1) * side, :side], right[k * side : (k + 1) * side, side:]], axis=0)
            for k in range(patches)
        ],
        axis=1,
    )
    back = dot3(bwd, split(regrouped))

    t_re = t_im = den = None
    for k in range(patches):
        o_re, o_im = objects[k]
        b_re, b_im = back[:side, k * side : (k + 1) * side], back[side:, k * side : (k + 1) * side]
        new = (o_re * b_re + o_im * b_im, o_re * b_im - o_im * b_re, o_re * o_re + o_im * o_im)
        t_re, t_im, den = new if k == 0 else (t_re + new[0], t_im + new[1], den + new[2])
    piece = side // n_tile
    for j in range(n_tile):
        here = slice(j * piece, (j + 1) * piece)
        terms[j, 0], terms[j, 1], terms[j, 2] = t_re[here], t_im[here], den[here]
    if inside:
        each_tile(
            lambda j: to(terms.at[j], terms_in.at[me_t], t_send.at[j], t_recv.at[me_t], tile=j).start()
        )

    strips = []
    for k, (_, col) in enumerate(places):
        b_re, b_im = back[:side, k * side : (k + 1) * side], back[side:, k * side : (k + 1) * side]
        grads = (probe_re * b_re + probe_im * b_im, probe_re * b_im - probe_im * b_re)
        high_low = jnp.concatenate(split(jnp.concatenate(grads, axis=0)), axis=0)
        moved = jnp.dot(high_low, chosen((side, width), col), preferred_element_type=F32).astype(BF16)
        strips.append(jnp.concatenate([moved[i * side : (i + 1) * side] for i in range(4)], axis=1))
    row_place = jnp.concatenate([chosen((rows + side, side), row, True) for row, _ in places], axis=1)
    placed = jnp.dot(row_place, jnp.concatenate(strips, axis=0), preferred_element_type=F32)
    for c in range(2):
        acc[c] = placed[:, c * width : (c + 1) * width] + placed[:, (c + 2) * width : (c + 3) * width]

    g_up = to(acc.at[:, 0:half], from_below, halo_send.at[2], halo_recv.at[2], tile=me_t - 1)
    g_down = to(acc.at[:, half + rows :], from_above, halo_send.at[3], halo_recv.at[3], tile=me_t + 1)
    pl.when(jnp.logical_not(first))(g_up.start)
    pl.when(jnp.logical_not(last))(g_down.start)

    def resample(values, spots):
        out = dot3(split(values), (det_hl[0], det_hl[1]), transposed=True)
        for c in range(2):
            for n, i in enumerate(spots):
                at = (c * len(spots) + n) * slab
                outbox[i, c] = out[at : at + slab]

    def send_slab(i):
        to(outbox.at[i], inbox.at[me_a], a2a_send.at[i], a2a_recv.at[me_a], angle=i).start()

    low, high = half // slab, (rows - half) // slab
    middle = slice(half, rows - half)
    for c in range(2):
        upd_ref[c, 0, middle] = pad[c, 2 * half : rows] - STEP_SIZE * acc[c, 2 * half : rows]
    resample(jnp.concatenate([upd_ref[0, 0, middle], upd_ref[1, 0, middle]], axis=0), range(low, high))
    each_angle(send_slab, low, high)

    if inside:
        each_tile(
            lambda j: to(terms.at[j], terms_in.at[j], t_send.at[j], t_recv.at[j], tile=j).wait()
        )
        terms_in[me_t] = terms[me_t]
        total = terms_in[0]
        for j in range(1, n_tile):
            total = total + terms_in[j]
        small = piece // n_ang
        for i in range(n_ang):
            parts[i] = total[:, i * small : (i + 1) * small]
        each_angle(
            lambda i: to(parts.at[i], parts_in.at[me_a], p_send.at[i], p_recv.at[me_a], angle=i).start()
        )

    pl.when(jnp.logical_not(last))(g_up.wait_recv)
    pl.when(jnp.logical_not(first))(g_down.wait_recv)
    for c in range(2):
        upd_ref[c, 0, :half] = pad[c, half : 2 * half] - STEP_SIZE * (acc[c, half : 2 * half] + from_above[c])
        upd_ref[c, 0, rows - half :] = pad[c, rows : rows + half] - STEP_SIZE * (
            acc[c, rows : rows + half] + from_below[c]
        )
    edges = [upd_ref[c, 0, s] for c in range(2) for s in (slice(0, half), slice(rows - half, rows))]
    resample(jnp.concatenate(edges, axis=0), [*range(low), *range(high, n_ang)])
    each_angle(send_slab, 0, low)
    each_angle(send_slab, high, n_ang)

    if inside:
        each_angle(lambda i: to(parts.at[i], parts_in.at[i], p_send.at[i], p_recv.at[i], angle=i).wait())
        parts_in[me_a] = parts[me_a]
        total = parts_in[0]
        for i in range(1, n_ang):
            total = total + parts_in[i]
        scale = lax.rsqrt(total[2] + EPSILON)
        dirs[me_a, 0] = total[0] * scale
        dirs[me_a, 1] = total[1] * scale
        each_angle(lambda i: to(dirs.at[me_a], dirs.at[me_a], d_send.at[i], d_recv.at[me_a], angle=i).start())
        each_angle(lambda i: to(dirs.at[me_a], dirs.at[i], d_send.at[i], d_recv.at[i], angle=i).wait())
        for i in range(n_ang):
            quarters[me_t, :, i * small : (i + 1) * small] = dirs[i]
        each_tile(
            lambda j: to(quarters.at[me_t], quarters.at[me_t], q_send.at[j], q_recv.at[me_t], tile=j).start()
        )

    inbox[me_a] = outbox[me_a]
    each_angle(lambda i: to(outbox.at[i], inbox.at[i], a2a_send.at[i], a2a_recv.at[i], angle=i).wait())
    for c in range(2):
        gathered = jnp.concatenate([inbox[i, c] for i in range(n_ang)], axis=0)
        out = dot3((mix_hl[0], mix_hl[1]), split(gathered))
        vol_ref[c, 0] = out.reshape(slab, n_reg, n_rad)

    if inside:
        each_tile(lambda j: to(quarters.at[me_t], quarters.at[j], q_send.at[j], q_recv.at[j], tile=j).wait())
        for j in range(n_tile):
            dir_ref[:, j * piece : (j + 1) * piece] = quarters[j]
    else:
        for j in range(n_tile):
            dir_ref[:, j * piece : (j + 1) * piece] = terms[j]

    pl.when(jnp.logical_not(first))(up.wait_send)
    pl.when(jnp.logical_not(last))(down.wait_send)
    pl.when(jnp.logical_not(first))(g_up.wait_send)
    pl.when(jnp.logical_not(last))(g_down.wait_send)


def local(
    projection, probe, amplitude, pos_row, pos_col, ang_offset, ang_weight, det_offset, det_weight
):
    n_ang, n_tile = lax.axis_size("angle"), lax.axis_size("tile")
    side, rows, width = probe.shape[-1], projection.shape[2], projection.shape[3]
    patches, n_reg, n_rad = amplitude.shape[1], ang_weight.shape[0], det_weight.shape[0]
    half, slab, piece = side // 2, rows // n_ang, side // n_tile
    inside = piece % n_ang == 0
    small = piece // n_ang if inside else 8
    sizes = (n_ang, n_tile, side, rows, width, patches, n_reg, n_rad, slab, inside)
    vmem = pl.BlockSpec(memory_space=pltpu.VMEM)
    smem = pl.BlockSpec(memory_space=pltpu.SMEM)
    dma = pltpu.SemaphoreType.DMA
    lead = 2 if inside else 3
    updated, direction, volume = pl.pallas_call(
        functools.partial(kernel, sizes),
        out_shape=(
            jax.ShapeDtypeStruct(projection.shape, F32),
            jax.ShapeDtypeStruct((lead, side, side), F32),
            jax.ShapeDtypeStruct((2, 1, slab, n_reg, n_rad), F32),
        ),
        in_specs=[pl.BlockSpec(memory_space=pl.ANY), vmem, vmem, smem, smem, vmem, vmem, vmem, vmem, vmem],
        out_specs=(vmem, vmem, vmem),
        scratch_shapes=[
            pltpu.VMEM((2, rows + side, width), F32),
            pltpu.VMEM((2, rows + side, width), F32),
            pltpu.VMEM((2, half, width), F32),
            pltpu.VMEM((2, half, width), F32),
            pltpu.VMEM((2, n_rad, width), BF16),
            pltpu.VMEM((2, slab * n_reg, n_ang * slab), BF16),
            pltpu.VMEM((n_ang, 2, slab, n_rad), F32),
            pltpu.VMEM((n_ang, 2, slab, n_rad), F32),
            pltpu.VMEM((n_tile, 3, piece, side), F32),
            pltpu.VMEM((n_tile, 3, piece, side), F32),
            pltpu.VMEM((n_ang, 3, small, side), F32),
            pltpu.VMEM((n_ang, 3, small, side), F32),
            pltpu.VMEM((n_ang, 2, small, side), F32),
            pltpu.VMEM((n_tile, 2, piece, side), F32),
            dma,
            dma((4,)),
            dma((4,)),
            dma((n_ang,)),
            dma((n_ang,)),
            dma((n_tile,)),
            dma((n_tile,)),
            dma((n_ang,)),
            dma((n_ang,)),
            dma((n_ang,)),
            dma((n_ang,)),
            dma((n_tile,)),
            dma((n_tile,)),
        ],
        compiler_params=pltpu.CompilerParams(
            collective_id=0, has_side_effects=True, vmem_limit_bytes=48 * 1024 * 1024
        ),
    )(
        projection,
        probe,
        amplitude,
        pos_row,
        pos_col,
        ang_offset,
        ang_weight,
        det_offset,
        det_weight,
        jnp.asarray(dft_tables(side)),
    )
    if not inside:
        sums = lax.psum(direction, ("angle", "tile"))
        direction = sums[:2] * lax.rsqrt(sums[2] + EPSILON)
    return (updated, direction, volume)


def solution(mesh):
    in_specs = (
        P(None, "angle", "tile", None),
        P(),
        P("angle", "tile", None, None),
        P("angle", "tile"),
        P("angle", "tile"),
        P(),
        P(),
        P(),
        P(),
    )
    out_specs = (P(None, "angle", "tile", None), P(), P(None, "tile", "angle", None, None))
    return jax.shard_map(local, mesh=mesh, in_specs=in_specs, out_specs=out_specs, check_vma=False)
```

```python
import functools
import math

import jax
import jax.numpy as jnp
import numpy as np
from jax import lax
from jax.experimental import pallas as pl
from jax.experimental.pallas import tpu as pltpu
from jax.sharding import PartitionSpec as P

STEP_SIZE = 0.1
EPSILON = 1e-06
MESH = pl.DeviceIdType.MESH
F32 = jnp.float32
BF16 = jnp.bfloat16


def dft_tables(length):
    counter = np.arange(length)
    angle = (counter[:, None] * counter[None, :] % length) * (2.0 * math.pi / length)
    re, im = np.cos(angle) / math.sqrt(length), -np.sin(angle) / math.sqrt(length)
    forward = np.block([[re, -im], [im, re]]).astype(np.float32)
    tables = []
    for table in (forward, forward.T):
        high = table.astype(jnp.bfloat16)
        tables += [high, (table - high.astype(np.float32)).astype(jnp.bfloat16)]
    return np.stack(tables)


def split(value):
    high = value.astype(BF16)
    return high, (value - high.astype(F32)).astype(BF16)


def dot3(left, right):
    one = functools.partial(jnp.dot, preferred_element_type=F32)
    return one(left[0], right[0]) + (one(left[0], right[1]) + one(left[1], right[0]))


def chosen(shape, by, from_rows=False):
    i, j = (lax.broadcasted_iota(jnp.int32, shape, d) for d in range(2))
    return jnp.where(i == j + by if from_rows else j == i + by, 1.0, 0.0).astype(BF16)


def quotient(value, by):
    if by & (by - 1) == 0:
        return lax.shift_right_logical(value, jnp.int32(by.bit_length() - 1))
    return lax.div(value, jnp.int32(by))


def as_column(row, count):
    shape = (count, count)
    diagonal = lax.broadcasted_iota(jnp.int32, shape, 0) == lax.broadcasted_iota(jnp.int32, shape, 1)
    wide = jnp.broadcast_to(row.astype(F32)[None, :], shape)
    return jnp.sum(jnp.where(diagonal, wide, 0.0), axis=1, keepdims=True)


def kernel(
    sizes,
    proj_ref,
    probe_ref,
    amp_ref,
    row_ref,
    col_ref,
    ang_off_ref,
    ang_w_ref,
    det_off_ref,
    det_w_ref,
    table_ref,
    upd_ref,
    dir_ref,
    vol_ref,
    pad,
    probe_v,
    amp_v,
    table_v,
    upd_v,
    acc,
    from_above,
    from_below,
    det_hl,
    mix_hl,
    outbox,
    inbox,
    terms,
    terms_in,
    parts,
    parts_in,
    dirs,
    quarters,
    local_sem,
    halo_send,
    halo_recv,
    a2a_send,
    a2a_recv,
    t_send,
    t_recv,
    p_send,
    p_recv,
    d_send,
    d_recv,
    q_send,
    q_recv,
):
    n_ang, n_tile, side, rows, width, patches, n_reg, n_rad, slab, inside = sizes
    half = side // 2
    me_a, me_t = lax.axis_index("angle"), lax.axis_index("tile")
    first, last = me_t == 0, me_t == n_tile - 1
    barrier = pltpu.get_barrier_semaphore()

    def each_angle(body, low=0, high=n_ang):
        def step(i, carry):
            @pl.when(i != me_a)
            def _():
                body(i)

            return carry

        lax.fori_loop(low, high, step, 0)

    def each_tile(body):
        for j in range(n_tile):

            @pl.when(j != me_t)
            def _():
                body(j)

    def to(src, dst, send, recv, angle=None, tile=None):
        return pltpu.make_async_remote_copy(
            src_ref=src,
            dst_ref=dst,
            send_sem=send,
            recv_sem=recv,
            device_id=(me_a if angle is None else angle, me_t if tile is None else tile),
            device_id_type=MESH,
        )

    def hello(angle, tile):
        pl.semaphore_signal(barrier, inc=1, device_id=(angle, tile), device_id_type=MESH)

    each_tile(lambda j: hello(me_a, j))
    each_angle(lambda i: hello(i, me_t))
    own = pltpu.make_async_copy(proj_ref.at[:, 0], pad.at[:, half : half + rows], local_sem.at[0])
    others = [
        pltpu.make_async_copy(probe_ref, probe_v, local_sem.at[1]),
        pltpu.make_async_copy(table_ref, table_v, local_sem.at[2]),
        pltpu.make_async_copy(amp_ref.at[0], amp_v, local_sem.at[3]),
    ]
    own.start()
    for copy in others:
        copy.start()

    det_rows = lax.broadcasted_iota(jnp.int32, (width, n_rad), 0)
    det = jnp.zeros((width, n_rad), F32)
    for step in range(det_w_ref.shape[0]):
        hits = det_rows == det_off_ref[...][None, :] + step
        det = det + jnp.where(hits, det_w_ref[step : step + 1, :], 0.0)
    det_hl[0], det_hl[1] = split(det)
    square = (slab * n_reg, n_ang * slab)
    wide_rows = lax.broadcasted_iota(jnp.int32, square, 0)
    wide_cols = lax.broadcasted_iota(jnp.int32, square, 1)
    source = quotient(wide_cols, slab)
    same = (wide_cols - source * slab) == quotient(wide_rows, n_reg)
    source = source.astype(F32)
    offs = jnp.concatenate([as_column(ang_off_ref[...], n_reg)] * slab, axis=0)
    mix = jnp.zeros(square, F32)
    for step in range(ang_w_ref.shape[0]):
        weight = jnp.concatenate([as_column(ang_w_ref[step], n_reg)] * slab, axis=0)
        mix = mix + jnp.where(source == offs + float(step), weight, 0.0)
    mix_hl[0], mix_hl[1] = split(jnp.where(same, mix, 0.0))
    for copy in others:
        copy.wait()
    pl.semaphore_wait(barrier, n_tile - 1 + n_ang - 1)

    up = to(proj_ref.at[:, 0, 0:half], pad.at[:, half + rows :], halo_send.at[0], halo_recv.at[0], tile=me_t - 1)
    down = to(
        proj_ref.at[:, 0, rows - half :], pad.at[:, 0:half], halo_send.at[1], halo_recv.at[1], tile=me_t + 1
    )
    pl.when(jnp.logical_not(first))(up.start)
    pl.when(jnp.logical_not(last))(down.start)

    @pl.when(first)
    def _():
        pad[:, 0:half] = jnp.zeros((2, half, width), F32)
        from_above[...] = jnp.zeros_like(from_above)

    @pl.when(last)
    def _():
        pad[:, half + rows :] = jnp.zeros((2, half, width), F32)
        from_below[...] = jnp.zeros_like(from_below)

    places = [(row_ref[0, k], col_ref[0, k]) for k in range(patches)]
    row_pick = jnp.concatenate([chosen((side, rows), row - half) for row, _ in places], axis=0)
    own.wait()
    seen = jnp.concatenate([pad[0, half : half + rows], pad[1, half : half + rows]], axis=1)
    inner = [jnp.dot(row_pick, part, preferred_element_type=F32) for part in split(seen)]
    edge_cols = lax.broadcasted_iota(jnp.int32, (side, side), 1)
    edge_cols = jnp.where(edge_cols < half, edge_cols, edge_cols + rows)
    edge_rows = lax.broadcasted_iota(jnp.int32, (side, side), 0)
    edge_pick = jnp.concatenate(
        [jnp.where(edge_cols == edge_rows + row, 1.0, 0.0).astype(BF16) for row, _ in places], axis=0
    )
    pl.when(jnp.logical_not(last))(up.wait_recv)
    pl.when(jnp.logical_not(first))(down.wait_recv)
    seen = [jnp.concatenate([pad[c, :half], pad[c, half + rows :]], axis=0) for c in range(2)]
    seen = split(jnp.concatenate(seen, axis=1))
    seen = [(i + jnp.dot(edge_pick, part, preferred_element_type=F32)).astype(BF16) for i, part in zip(inner, seen)]
    probe_re, probe_im = probe_v[0], probe_v[1]
    objects, exits = [], []
    for k, (_, col) in enumerate(places):
        here = slice(k * side, (k + 1) * side)
        strip = jnp.concatenate([part[here, c * width : (c + 1) * width] for part in seen for c in range(2)], axis=0)
        picked = jnp.dot(strip, chosen((width, side), col, True), preferred_element_type=F32)
        o_re, o_im = [picked[c * side : (c + 1) * side] + picked[(c + 2) * side : (c + 3) * side] for c in range(2)]
        objects.append((o_re, o_im))
        exits.append(
            jnp.concatenate([probe_re * o_re - probe_im * o_im, probe_re * o_im + probe_im * o_re], axis=0)
        )
    fwd = (table_v[0], table_v[1])
    bwd = (table_v[2], table_v[3])
    left = dot3(fwd, split(jnp.concatenate(exits, axis=1)))
    stacked = jnp.concatenate(
        [
            jnp.concatenate([left[:side, k * side : (k + 1) * side], left[side:, k * side : (k + 1) * side]], axis=1)
            for k in range(patches)
        ],
        axis=0,
    )
    spec = dot3(split(stacked), bwd)
    s_re, s_im = spec[:, :side], spec[:, side:]
    amp = amp_v[...].reshape(patches * side, side)
    factor = 1.0 - amp / jnp.maximum(jnp.sqrt(s_re * s_re + s_im * s_im), 1.0)
    right = dot3(split(jnp.concatenate([s_re * factor, s_im * factor], axis=1)), fwd)
    regrouped = jnp.concatenate(
        [
            jnp.concatenate([right[k * side : (k + 1) * side, :side], right[k * side : (k + 1) * side, side:]], axis=0)
            for k in range(patches)
        ],
        axis=1,
    )
    back = dot3(bwd, split(regrouped))

    t_re = t_im = den = None
    for k in range(patches):
        o_re, o_im = objects[k]
        b_re, b_im = back[:side, k * side : (k + 1) * side], back[side:, k * side : (k + 1) * side]
        new = (o_re * b_re + o_im * b_im, o_re * b_im - o_im * b_re, o_re * o_re + o_im * o_im)
        t_re, t_im, den = new if k == 0 else (t_re + new[0], t_im + new[1], den + new[2])
    piece = side // n_tile
    for j in range(n_tile):
        here = slice(j * piece, (j + 1) * piece)
        terms[j, 0], terms[j, 1], terms[j, 2] = t_re[here], t_im[here], den[here]
    if inside:
        each_tile(
            lambda j: to(terms.at[j], terms_in.at[me_t], t_send.at[j], t_recv.at[me_t], tile=j).start()
        )

    strips = []
    for k, (_, col) in enumerate(places):
        b_re, b_im = back[:side, k * side : (k + 1) * side], back[side:, k * side : (k + 1) * side]
        grads = (probe_re * b_re + probe_im * b_im, probe_re * b_im - probe_im * b_re)
        high_low = jnp.concatenate(split(jnp.concatenate(grads, axis=0)), axis=0)
        moved = jnp.dot(high_low, chosen((side, width), col), preferred_element_type=F32).astype(BF16)
        strips.append(jnp.concatenate([moved[i * side : (i + 1) * side] for i in range(4)], axis=1))
    row_place = jnp.concatenate([chosen((rows + side, side), row, True) for row, _ in places], axis=1)
    placed = jnp.dot(row_place, jnp.concatenate(strips, axis=0), preferred_element_type=F32)
    for c in range(2):
        acc[c] = placed[:, c * width : (c + 1) * width] + placed[:, (c + 2) * width : (c + 3) * width]

    g_up = to(acc.at[:, 0:half], from_below, halo_send.at[2], halo_recv.at[2], tile=me_t - 1)
    g_down = to(acc.at[:, half + rows :], from_above, halo_send.at[3], halo_recv.at[3], tile=me_t + 1)
    pl.when(jnp.logical_not(first))(g_up.start)
    pl.when(jnp.logical_not(last))(g_down.start)

    def resample(values, spots):
        out = dot3(split(values), (det_hl[0], det_hl[1]))
        for c in range(2):
            for n, i in enumerate(spots):
                at = (c * len(spots) + n) * slab
                outbox[i, c] = out[at : at + slab]

    def send_slab(i):
        to(outbox.at[i], inbox.at[me_a], a2a_send.at[i], a2a_recv.at[me_a], angle=i).start()

    low, high = half // slab, (rows - half) // slab
    middle = slice(half, rows - half)
    for c in range(2):
        upd_v[c, middle] = pad[c, 2 * half : rows] - STEP_SIZE * acc[c, 2 * half : rows]
    resample(jnp.concatenate([upd_v[0, middle], upd_v[1, middle]], axis=0), range(low, high))
    if inside:
        each_tile(
            lambda j: to(terms.at[j], terms_in.at[j], t_send.at[j], t_recv.at[j], tile=j).wait()
        )
        terms_in[me_t] = terms[me_t]
        total = terms_in[0]
        for j in range(1, n_tile):
            total = total + terms_in[j]
        small = piece // n_ang
        for i in range(n_ang):
            parts[i] = total[:, i * small : (i + 1) * small]
        each_angle(
            lambda i: to(parts.at[i], parts_in.at[me_a], p_send.at[i], p_recv.at[me_a], angle=i).start()
        )
    each_angle(send_slab, low, high)

    if inside:
        each_angle(lambda i: to(parts.at[i], parts_in.at[i], p_send.at[i], p_recv.at[i], angle=i).wait())
        parts_in[me_a] = parts[me_a]
        total = parts_in[0]
        for i in range(1, n_ang):
            total = total + parts_in[i]
        scale = lax.rsqrt(total[2] + EPSILON)
        dirs[me_a, 0] = total[0] * scale
        dirs[me_a, 1] = total[1] * scale
        each_angle(lambda i: to(dirs.at[me_a], dirs.at[me_a], d_send.at[i], d_recv.at[me_a], angle=i).start())

    pl.when(jnp.logical_not(last))(g_up.wait_recv)
    pl.when(jnp.logical_not(first))(g_down.wait_recv)
    for c in range(2):
        upd_v[c, :half] = pad[c, half : 2 * half] - STEP_SIZE * (acc[c, half : 2 * half] + from_above[c])
        upd_v[c, rows - half :] = pad[c, rows : rows + half] - STEP_SIZE * (
            acc[c, rows : rows + half] + from_below[c]
        )
    edges = [upd_v[c, s] for c in range(2) for s in (slice(0, half), slice(rows - half, rows))]
    resample(jnp.concatenate(edges, axis=0), [*range(low), *range(high, n_ang)])
    each_angle(send_slab, 0, low)
    each_angle(send_slab, high, n_ang)

    out_copy = pltpu.make_async_copy(upd_v, upd_ref.at[:, 0], local_sem.at[4])
    out_copy.start()
    if inside:
        each_angle(lambda i: to(dirs.at[me_a], dirs.at[i], d_send.at[i], d_recv.at[i], angle=i).wait())
        for i in range(n_ang):
            quarters[me_t, :, i * small : (i + 1) * small] = dirs[i]
        each_tile(
            lambda j: to(quarters.at[me_t], quarters.at[me_t], q_send.at[j], q_recv.at[me_t], tile=j).start()
        )

    inbox[me_a] = outbox[me_a]
    each_angle(lambda i: to(outbox.at[i], inbox.at[i], a2a_send.at[i], a2a_recv.at[i], angle=i).wait())
    for c in range(2):
        gathered = jnp.concatenate([inbox[i, c] for i in range(n_ang)], axis=0)
        out = dot3((mix_hl[0], mix_hl[1]), split(gathered))
        vol_ref[c, 0] = out.reshape(slab, n_reg, n_rad)

    if inside:
        each_tile(lambda j: to(quarters.at[me_t], quarters.at[j], q_send.at[j], q_recv.at[j], tile=j).wait())
        for j in range(n_tile):
            dir_ref[:, j * piece : (j + 1) * piece] = quarters[j]
    else:
        for j in range(n_tile):
            dir_ref[:, j * piece : (j + 1) * piece] = terms[j]

    out_copy.wait()
    pl.when(jnp.logical_not(first))(up.wait_send)
    pl.when(jnp.logical_not(last))(down.wait_send)
    pl.when(jnp.logical_not(first))(g_up.wait_send)
    pl.when(jnp.logical_not(last))(g_down.wait_send)


def hand_over(upd_in, dir_in, vol_in, upd_out, dir_out, vol_out, sem):
    copies = []
    for n, (src, dst, axis, cuts) in enumerate(((upd_in, upd_out, 2, 2), (vol_in, vol_out, 2, 1), (dir_in, dir_out, 1, 1))):
        length = src.shape[axis] // cuts
        for c in range(2):
            for m in range(cuts):
                at = (slice(c, c + 1),) + (slice(None),) * (axis - 1) + (slice(m * length, (m + 1) * length),)
                copies.append(pltpu.make_async_copy(src.at[at], dst.at[at], sem.at[n, c * cuts + m]))
    for copy in copies:
        copy.start()
    for copy in copies:
        copy.wait()


def local(
    projection, probe, amplitude, pos_row, pos_col, ang_offset, ang_weight, det_offset, det_weight
):
    n_ang, n_tile = lax.axis_size("angle"), lax.axis_size("tile")
    side, rows, width = probe.shape[-1], projection.shape[2], projection.shape[3]
    patches, n_reg, n_rad = amplitude.shape[1], ang_weight.shape[0], det_weight.shape[0]
    half, slab, piece = side // 2, rows // n_ang, side // n_tile
    inside = piece % n_ang == 0
    small = piece // n_ang if inside else 8
    sizes = (n_ang, n_tile, side, rows, width, patches, n_reg, n_rad, slab, inside)
    vmem = pl.BlockSpec(memory_space=pltpu.VMEM)
    hbm = pl.BlockSpec(memory_space=pl.ANY)
    smem = pl.BlockSpec(memory_space=pltpu.SMEM)
    dma = pltpu.SemaphoreType.DMA
    lead = 2 if inside else 3
    updated, direction, volume = pl.pallas_call(
        functools.partial(kernel, sizes),
        out_shape=(
            jax.ShapeDtypeStruct(projection.shape, F32),
            jax.ShapeDtypeStruct((lead, side, side), F32),
            jax.ShapeDtypeStruct((2, 1, slab, n_reg, n_rad), F32),
        ),
        in_specs=[hbm, hbm, hbm, smem, smem, vmem, vmem, vmem, vmem, hbm],
        out_specs=(hbm, vmem, vmem),
        scratch_shapes=[
            pltpu.VMEM((2, rows + side, width), F32),
            pltpu.VMEM((2, side, side), F32),
            pltpu.VMEM((patches, side, side), F32),
            pltpu.VMEM((4, 2 * side, 2 * side), BF16),
            pltpu.VMEM((2, rows, width), F32),
            pltpu.VMEM((2, rows + side, width), F32),
            pltpu.VMEM((2, half, width), F32),
            pltpu.VMEM((2, half, width), F32),
            pltpu.VMEM((2, width, n_rad), BF16),
            pltpu.VMEM((2, slab * n_reg, n_ang * slab), BF16),
            pltpu.VMEM((n_ang, 2, slab, n_rad), F32),
            pltpu.VMEM((n_ang, 2, slab, n_rad), F32),
            pltpu.VMEM((n_tile, 3, piece, side), F32),
            pltpu.VMEM((n_tile, 3, piece, side), F32),
            pltpu.VMEM((n_ang, 3, small, side), F32),
            pltpu.VMEM((n_ang, 3, small, side), F32),
            pltpu.VMEM((n_ang, 2, small, side), F32),
            pltpu.VMEM((n_tile, 2, piece, side), F32),
            dma((5,)),
            dma((4,)),
            dma((4,)),
            dma((n_ang,)),
            dma((n_ang,)),
            dma((n_tile,)),
            dma((n_tile,)),
            dma((n_ang,)),
            dma((n_ang,)),
            dma((n_ang,)),
            dma((n_ang,)),
            dma((n_tile,)),
            dma((n_tile,)),
        ],
        compiler_params=pltpu.CompilerParams(
            collective_id=0, has_side_effects=True, vmem_limit_bytes=60 * 1024 * 1024
        ),
    )(
        projection,
        probe,
        amplitude,
        pos_row,
        pos_col,
        ang_offset,
        ang_weight.T,
        det_offset,
        det_weight.T,
        jnp.asarray(dft_tables(side)),
    )
    if not inside:
        sums = lax.psum(direction, ("angle", "tile"))
        direction = sums[:2] * lax.rsqrt(sums[2] + EPSILON)
        return (updated, direction, volume)
    results = (updated, direction, volume)
    return pl.pallas_call(
        hand_over,
        out_shape=[jax.ShapeDtypeStruct(r.shape, F32) for r in results],
        in_specs=[hbm] * 3,
        out_specs=[hbm] * 3,
        scratch_shapes=[dma((3, 4))],
        compiler_params=pltpu.CompilerParams(vmem_limit_bytes=60 * 1024 * 1024),
    )(*results)


def solution(mesh):
    in_specs = (
        P(None, "angle", "tile", None),
        P(),
        P("angle", "tile", None, None),
        P("angle", "tile"),
        P("angle", "tile"),
        P(),
        P(),
        P(),
        P(),
    )
    out_specs = (P(None, "angle", "tile", None), P(), P(None, "tile", "angle", None, None))
    return jax.shard_map(local, mesh=mesh, in_specs=in_specs, out_specs=out_specs, check_vma=False)
```
